128 devices in a mesh: ao: 16 (over y, x), aux: 8 (over z, core).
Axes of the slice: x: 4, y: 4, z: 4, core: 2. Of those that a mesh axis runs over, the one named last changes fastest.
Arguments:
- three_centre: bfloat16 [128, 1024, 1024], P('aux', 'ao'), may hold values from -0.26367188 to 0.26367188
- tensor_mask: int32 [16, 16], P('ao'), may hold values 0 or 1
- occ_density: bfloat16 [2, 1024, 1024], P(None, 'ao'), may hold values from -0.1875 to 0.1875
- virt_density: bfloat16 [2, 1024, 1024], P(None, 'ao'), may hold values from -0.1875 to 0.1875
- density_mask: int32 [2, 16, 16], P(None, 'ao'), may hold values 0 or 1
Outputs:
- response: float32 [2, 128, 128], P(None, 'aux', 'ao')
The draws below stay inside these ranges and needn't reach their ends.
All inputs are finite; a program needn't handle non-finite values. No bound on the sum of `tensor_mask` or of `density_mask` on one device may be relied on, other than what follows from the above.
Results may differ from the reference program's by a relative error of at most 0.0041.
Values may be sent and summed in bfloat16 or wider, within the bound.
No kernel may reach another device: no remote copies, remote signals or barrier semaphores. Data moves between devices by JAX's collectives and lax.ppermute only.
A program may use at most 128 MiB of HBM per device.

```python
import jax
import jax.numpy as jnp
from jax import lax

BS = 64
NB = 16
A = 1024
PAUX = 128


def plant(entries, key, smallest, top_value):
    longest = entries.shape.index(max(entries.shape))
    spots = []
    for shift in (0, 1):
        where = [jax.random.randint(jax.random.fold_in(key, axis), (), 0, length) for axis, length in enumerate(entries.shape)]
        where[longest] = (where[longest] + shift) % entries.shape[longest]
        spots.append(tuple(where))
    return entries.at[spots[0]].set(smallest).at[spots[1]].set(top_value)


def levels(own_key, shape, split, smallest, top_value):
    def one(axis_at, parts):
        draws = jax.random.uniform(jax.random.fold_in(jax.random.fold_in(own_key, 6), axis_at), (parts,), jnp.float32, smallest / len(split), top_value / len(split))
        return jnp.repeat(jnp.exp(draws), shape[axis_at] // parts).reshape((-1,) + (1,) * (len(shape) - axis_at - 1))

    factor_of = one(*split[0])
    for cut in split[1:]:
        factor_of = factor_of * one(*cut)
    return factor_of


def bell_draw(own_key, dims, width, limit, shards=(), dtype=jnp.bfloat16):
    entries = width * jax.random.normal(own_key, dims, jnp.float32)
    if shards:
        entries = entries * levels(own_key, dims, shards, -0.22, 0.18)
    return jnp.clip(entries, -limit, limit).astype(dtype)


def setup_inputs(seed: int = 0) -> dict:
    key_of = jax.random.split(jax.random.key(seed), 6)
    three_centre = bell_draw(key_of[0], (PAUX, A, A), ((2.0 / A) ** 0.5), 0.26367188, ((0, 8), (1, 16)))
    tensor_mask = plant((jax.random.randint(key_of[1], (NB, NB), 0, 4) < 3).astype(jnp.int32), jax.random.fold_in(key_of[1], 1), 0, 1)
    occ_density = bell_draw(key_of[2], (2, A, A), A ** -0.5, 0.1875, ((1, 16),))
    virt_density = bell_draw(key_of[3], (2, A, A), A ** -0.5, 0.1875, ((1, 16),))
    density_mask = plant((jax.random.randint(key_of[4], (2, NB, NB), 0, 4) < 3).astype(jnp.int32), jax.random.fold_in(key_of[4], 1), 0, 1)
    return dict(three_centre=three_centre, tensor_mask=tensor_mask, occ_density=occ_density, virt_density=virt_density, density_mask=density_mask)


def expand(mask_rows):
    grown = jnp.repeat(jnp.repeat(mask_rows, BS, axis=0), BS, axis=1)
    return grown.astype(jnp.bfloat16)


def reference(three_centre, tensor_mask, occ_density, virt_density, density_mask):
    screened = three_centre * expand(tensor_mask)[None]
    occ_mask = expand(density_mask[0])
    virt_mask = expand(density_mask[1])
    occ = occ_density * occ_mask[None]
    virt = virt_density * virt_mask[None]
    screened_wide = screened.astype(jnp.float32)
    groups = PAUX // 8
    blocks = screened.reshape(groups, 8, A, A)
    results = []
    for moment in range(2):
        occ_wide = occ[moment].astype(jnp.float32)
        virt_wide = virt[moment].astype(jnp.float32)

        def per_block(block):
            half = jnp.einsum("pmn,ns->pms", block.astype(jnp.float32), virt_wide).astype(jnp.bfloat16)
            paired = jnp.einsum("lm,pms->pls", occ_wide, half.astype(jnp.float32)).astype(jnp.bfloat16)
            return jnp.einsum("pls,qls->pq", paired.astype(jnp.float32), screened_wide)

        rows_out = lax.map(per_block, blocks)
        results.append(rows_out.reshape(PAUX, PAUX))
    return jnp.stack(results)
```

```python
import jax
import jax.numpy as jnp
from jax import lax
from jax.sharding import PartitionSpec as P

ALL = ("ao", "aux")


def expand(mask_row, width):
    return jnp.repeat(mask_row, width, axis=-1).astype(jnp.bfloat16)


def body(three_centre, tensor_mask, occ_density, virt_density, density_mask):
    per_group, rows, width = three_centre.shape
    blocks = width // rows
    devices = lax.axis_size("ao") * lax.axis_size("aux")
    groups = lax.axis_size("aux")
    slab = width // devices
    moment = lax.axis_index("aux") % 2
    other_core = [(a, a ^ 1) for a in range(groups)]

    screened = three_centre * expand(tensor_mask[0], rows)[None, None, :]
    dens_mask = expand(density_mask[:, 0, :], rows)
    occ_rows = lax.dynamic_index_in_dim(occ_density, moment, 0, False) * dens_mask[0][None, :]
    virt_rows = lax.dynamic_index_in_dim(virt_density, moment, 0, False) * dens_mask[1][None, :]
    dens = lax.all_gather(jnp.stack([virt_rows, occ_rows]), "ao", axis=1, tiled=True)
    virt, occ = dens[0], dens[1]

    own = lax.all_to_all(screened, "ao", split_axis=0, concat_axis=1, tiled=True)[0]
    twin = lax.ppermute(own, "aux", other_core)
    tensor_slab = lax.all_to_all(
        screened.reshape(per_group, groups, slab, width), "aux", split_axis=1, concat_axis=0, tiled=True
    ).reshape(-1, slab, width)

    partials = []
    for matrix in (own, twin):
        half = jnp.dot(matrix, virt, preferred_element_type=jnp.float32).astype(jnp.bfloat16)
        paired = jnp.dot(occ, half, preferred_element_type=jnp.float32).astype(jnp.bfloat16)
        got = lax.all_to_all(
            paired.reshape(devices, slab, width), ALL, split_axis=0, concat_axis=0, tiled=True
        )
        part = lax.dot_general(
            got, tensor_slab, (((1, 2), (1, 2)), ((), ())), preferred_element_type=jnp.float32
        )
        partials.append(part.reshape(blocks, groups // 2, 2, blocks, -1))
    mine, theirs = partials
    first = jnp.stack([mine[:, :, 0], theirs[:, :, 0]], axis=2)
    second = jnp.stack([theirs[:, :, 1], mine[:, :, 1]], axis=2)
    both = jnp.stack([first, second])
    parcels = jnp.transpose(both, (4, 2, 3, 0, 1, 5)).reshape(devices, -1)
    summed = lax.all_to_all(parcels, ALL, split_axis=0, concat_axis=0, tiled=True).sum(axis=0)
    return summed.reshape(2, per_group, -1)


def solution(mesh):
    return jax.shard_map(
        body,
        mesh=mesh,
        in_specs=(
            P("aux", "ao", None),
            P("ao", None),
            P(None, "ao", None),
            P(None, "ao", None),
            P(None, "ao", None),
        ),
        out_specs=P(None, "aux", "ao"),
        check_vma=False,
    )
```

```python
import jax
import jax.numpy as jnp
from jax import lax
from jax.sharding import PartitionSpec as P

ALL = ("ao", "aux")
SIDE = 4
CORES = 2


def expand(mask_row, width):
    return jnp.repeat(mask_row, width, axis=-1).astype(jnp.bfloat16)


def along_x(step):
    return [(i, (i // SIDE) * SIDE + (i % SIDE + step) % SIDE) for i in range(SIDE * SIDE)]


def along_y(step):
    return [(i, ((i // SIDE + step) % SIDE) * SIDE + i % SIDE) for i in range(SIDE * SIDE)]


def along_z(step):
    return [(k, ((k // CORES + step) % SIDE) * CORES + k % CORES) for k in range(SIDE * CORES)]


OTHER_CORE = [(k, k ^ 1) for k in range(SIDE * CORES)]
SAME_CORE = [
    [i * SIDE * CORES + CORES * z + core for i in range(SIDE * SIDE) for z in range(SIDE)]
    for core in range(CORES)
]
OFFSETS = (0, -1, 1, 2)


def ring(rows, step):
    before = lax.ppermute(rows, "ao", step(1))
    after = lax.ppermute(rows, "ao", step(-1))
    far = lax.ppermute(after, "ao", step(-1))
    return rows, before, after, far


def place(pieces, spot):
    whole = jnp.zeros((SIDE,) + pieces[0].shape, pieces[0].dtype)
    for offset, piece in zip(OFFSETS, pieces):
        whole = lax.dynamic_update_index_in_dim(whole, piece, (spot + offset) % SIDE, 0)
    return whole


def body(three_centre, tensor_mask, occ_density, virt_density, density_mask):
    per_group, rows, width = three_centre.shape
    chips = SIDE**3
    slab = width // chips
    spot = lax.axis_index("ao")
    x, y = spot % SIDE, spot // SIDE
    z, core = lax.axis_index("aux") // CORES, lax.axis_index("aux") % CORES

    dens_mask = expand(density_mask[:, 0, :], rows)
    virt_rows = lax.dynamic_index_in_dim(virt_density, core, 0, False) * dens_mask[1][None, :]
    occ_rows = lax.dynamic_index_in_dim(occ_density, core, 0, False) * dens_mask[0][None, :]
    virt_near = ring(virt_rows, along_x)
    occ_near = ring(occ_rows, along_y)
    virt_row = jnp.concatenate(virt_near, 0)
    occ_row = jnp.concatenate(occ_near, 0)
    virt_far = ring(virt_row, along_y)
    occ_far = ring(occ_row, along_x)
    virt = place([place(list(v.reshape(SIDE, rows, width)), x) for v in virt_far], y)
    occ = place([place(list(o.reshape(SIDE, rows, width)), y) for o in occ_far], x)
    virt = virt.reshape(width, width)
    occ = jnp.swapaxes(occ, 0, 1).reshape(width, width)

    screened = three_centre * expand(tensor_mask[0], rows)[None, None, :]
    own = lax.all_to_all(screened, "ao", split_axis=0, concat_axis=1, tiled=True)[0]
    twin = lax.ppermute(own, "aux", OTHER_CORE)

    def cut(offset):
        view = screened.reshape(per_group, SIDE, slab, width)
        return lax.dynamic_index_in_dim(view, (z + offset) % SIDE, 1, False)

    far, cut_at = cut(2), per_group // 2
    before = lax.ppermute(jnp.concatenate([cut(1), far[:cut_at]]), "aux", along_z(1))
    after = lax.ppermute(jnp.concatenate([cut(-1), far[cut_at:]]), "aux", along_z(-1))
    opposite = jnp.concatenate(
        [
            lax.ppermute(before[per_group:], "aux", along_z(1)),
            lax.ppermute(after[per_group:], "aux", along_z(-1)),
        ]
    )
    slabs = place([cut(0), before[:per_group], after[:per_group], opposite], z)
    slabs_twin = lax.ppermute(slabs, "aux", OTHER_CORE)
    tensor_slab = jnp.where(
        core == 0, jnp.stack([slabs, slabs_twin], 1), jnp.stack([slabs_twin, slabs], 1)
    ).reshape(-1, slab, width)

    products = []
    for matrix in (own, twin):
        half = jnp.dot(matrix, virt, preferred_element_type=jnp.float32).astype(jnp.bfloat16)
        paired = jnp.dot(occ, half, preferred_element_type=jnp.float32).astype(jnp.bfloat16)
        products.append(paired.reshape(chips, slab, width))
    got = lax.all_to_all(
        jnp.stack(products, 1), ALL, split_axis=0, concat_axis=0, tiled=True, axis_index_groups=SAME_CORE
    )
    part = lax.dot_general(
        got, tensor_slab, (((2, 3), (1, 2)), ((), ())), preferred_element_type=jnp.float32
    )
    part = part.reshape(SIDE * SIDE, SIDE, CORES, SIDE * SIDE, -1)
    parcels = jnp.transpose(part, (3, 1, 2, 0, 4)).reshape(chips, -1)
    summed = lax.all_to_all(
        parcels, ALL, split_axis=0, concat_axis=0, tiled=True, axis_index_groups=SAME_CORE
    ).sum(axis=0).reshape(CORES, per_group, -1)
    mine, theirs = summed[0], lax.ppermute(summed[1], "aux", OTHER_CORE)
    return jnp.where(core == 0, jnp.stack([mine, theirs]), jnp.stack([theirs, mine]))


def solution(mesh):
    return jax.shard_map(
        body,
        mesh=mesh,
        in_specs=(
            P("aux", "ao", None),
            P("ao", None),
            P(None, "ao", None),
            P(None, "ao", None),
            P(None, "ao", None),
        ),
        out_specs=P(None, "aux", "ao"),
        check_vma=False,
    )
```

```python
import jax
import jax.numpy as jnp
from jax import lax
from jax.experimental import pallas as pl
from jax.experimental.pallas import tpu as pltpu
from jax.sharding import PartitionSpec as P

ALL = ("ao", "aux")
SIDE = 4
CORES = 2
OFFSETS = (0, -1, 1, 2)
MIB = 1 << 20
LANES = 128

OTHER_CORE = [(k, k ^ 1) for k in range(SIDE * CORES)]
SAME_CORE = [
    [i * SIDE * CORES + CORES * z + core for i in range(SIDE * SIDE) for z in range(SIDE)]
    for core in range(CORES)
]


def expand(mask_row, width):
    return jnp.repeat(mask_row, width, axis=-1).astype(jnp.bfloat16)


def in_plane(step, swapped):
    pairs = []
    for i in range(SIDE * SIDE):
        x, y = i % SIDE, i // SIDE
        for k in range(SIDE * CORES):
            if (k % CORES == 1) != swapped:
                to = ((y + step) % SIDE) * SIDE + x
            else:
                to = y * SIDE + (x + step) % SIDE
            pairs.append((i * SIDE * CORES + k, to * SIDE * CORES + k))
    return pairs


def along_z(step):
    return [(k, ((k // CORES + step) % SIDE) * CORES + k % CORES) for k in range(SIDE * CORES)]


def ring(rows, swapped):
    before = lax.ppermute(rows, ALL, in_plane(1, swapped))
    after = lax.ppermute(rows, ALL, in_plane(-1, swapped))
    far = lax.ppermute(after, ALL, in_plane(-1, swapped))
    return rows, before, after, far


def hold(value, *others):
    def kernel(*refs):
        pass

    whole = pl.BlockSpec(memory_space=pl.ANY)
    return pl.pallas_call(
        kernel,
        out_shape=jax.ShapeDtypeStruct(value.shape, value.dtype),
        in_specs=[whole] * (1 + len(others)),
        out_specs=whole,
        input_output_aliases={0: 0},
    )(value, *others)


def occ_product(matrix, pieces, into, index):
    depth, width = matrix.shape
    chips, _, slab, _ = into if isinstance(into, tuple) else into.shape
    rows = depth // SIDE**2
    columns = width // 4
    first = isinstance(into, tuple)

    def kernel(matrix_ref, *refs):
        piece_refs, (out_ref, occ, sems) = refs[:SIDE], refs[-3:]

        @pl.when(pl.program_id(0) == 0)
        def _():
            spot = lax.axis_index("ao")
            core = lax.axis_index("aux") % CORES
            x, y = spot % SIDE, spot // SIDE
            outer, inner = jnp.where(core == 0, y, x), jnp.where(core == 0, x, y)
            outer_step, inner_step = jnp.where(core == 0, SIDE, 1), jnp.where(core == 0, 1, SIDE)
            copies = []
            for g in range(SIDE):
                for k in range(SIDE):
                    block = ((outer + OFFSETS[g] + SIDE) % SIDE) * outer_step
                    block += ((inner + OFFSETS[k] + SIDE) % SIDE) * inner_step
                    copies.append(
                        pltpu.make_async_copy(
                            piece_refs[g].at[pl.ds(k * rows, rows)],
                            occ.at[pl.ds(pl.multiple_of(block * rows, rows), rows)],
                            sems.at[g * SIDE + k],
                        )
                    )
            for copy in copies:
                copy.start()
            for copy in copies:
                copy.wait()

        product = jnp.dot(occ[...], matrix_ref[...], preferred_element_type=jnp.float32)
        out_ref[...] = product.astype(jnp.bfloat16).reshape(out_ref.shape)

    anywhere = pl.BlockSpec(memory_space=pl.ANY)
    shape = into if first else into.shape
    return pl.pallas_call(
        kernel,
        grid=(width // columns,),
        out_shape=jax.ShapeDtypeStruct(shape, jnp.bfloat16),
        in_specs=[pl.BlockSpec((depth, columns), lambda j: (0, j))]
        + [anywhere] * SIDE
        + ([] if first else [anywhere]),
        out_specs=pl.BlockSpec((chips, 1, slab, columns), lambda j: (0, index, 0, j)),
        scratch_shapes=[
            pltpu.VMEM((depth, width), jnp.bfloat16),
            pltpu.SemaphoreType.DMA((SIDE * SIDE,)),
        ],
        input_output_aliases={} if first else {1 + SIDE: 0},
        compiler_params=pltpu.CompilerParams(vmem_limit_bytes=40 * MIB),
        cost_estimate=pl.CostEstimate(
            flops=2 * depth * depth * width, bytes_accessed=6 * depth * width, transcendentals=0
        ),
    )(matrix, *pieces, *([] if first else [into]))


def final_product(got, other):
    sources, pair, slab, width = got.shape
    count = other.shape[-1]
    columns = width // 4

    def kernel(got_ref, other_ref, out_ref, wide):
        total = jnp.zeros(out_ref.shape, jnp.float32)
        for part in range(columns // LANES):
            lanes = pl.ds(part * LANES, LANES)
            wide[part] = got_ref[..., lanes].reshape(wide.shape[1:]).astype(jnp.float32)
        for row in range(slab):
            left = [wide[part, pl.ds(row, sources * pair, stride=slab), :] for part in range(columns // LANES)]
            left = jnp.concatenate(left, 1).astype(jnp.bfloat16)
            total += jnp.dot(left, other_ref[row], preferred_element_type=jnp.float32)

        @pl.when(pl.program_id(0) == 0)
        def _():
            out_ref[...] = jnp.zeros_like(out_ref)

        out_ref[...] += total

    return pl.pallas_call(
        kernel,
        grid=(width // columns,),
        out_shape=jax.ShapeDtypeStruct((sources * pair, count), jnp.float32),
        in_specs=[
            pl.BlockSpec((sources, pair, slab, columns), lambda j: (0, 0, 0, j)),
            pl.BlockSpec((slab, columns, count), lambda j: (0, j, 0)),
        ],
        out_specs=pl.BlockSpec((sources * pair, count), lambda j: (0, 0)),
        scratch_shapes=[pltpu.VMEM((columns // LANES, sources * pair * slab, LANES), jnp.float32)],
        compiler_params=pltpu.CompilerParams(vmem_limit_bytes=40 * MIB),
        cost_estimate=pl.CostEstimate(
            flops=2 * sources * pair * slab * width * count,
            bytes_accessed=2 * got.size + 2 * other.size,
            transcendentals=0,
        ),
    )(got, other)


def body(three_centre, tensor_mask, occ_density, virt_density, density_mask):
    per_group, rows, width = three_centre.shape
    chips = SIDE**3
    slab = width // chips
    z, core = lax.axis_index("aux") // CORES, lax.axis_index("aux") % CORES

    dens_mask = expand(density_mask[:, 0, :], rows)
    row_mask = expand(tensor_mask[0], rows)
    occ_rows = lax.dynamic_index_in_dim(occ_density, core, 0, False) * dens_mask[0][None, :]
    virt_rows = lax.dynamic_index_in_dim(virt_density, core, 0, False) * dens_mask[1][None, :]

    occ_line = jnp.concatenate(ring(occ_rows, False), 0)
    occ_pieces = ring(occ_line, True)

    def cut(offset):
        view = three_centre.reshape(per_group, SIDE, slab, width)
        return lax.dynamic_index_in_dim(view, (z + offset) % SIDE, 1, False) * row_mask

    far, cut_at = cut(2), per_group // 2
    before = lax.ppermute(jnp.concatenate([cut(1), far[:cut_at]]), "aux", along_z(1))
    after = lax.ppermute(jnp.concatenate([cut(3), far[cut_at:]]), "aux", along_z(-1))
    far_a = lax.ppermute(before[per_group:], "aux", along_z(1))
    far_b = lax.ppermute(after[per_group:], "aux", along_z(-1))

    screened = hold(three_centre * row_mask, *occ_pieces[1:], far_a, far_b)
    own = lax.all_to_all(screened, "ao", split_axis=0, concat_axis=1, tiled=True)[0]
    twin = lax.ppermute(own, "aux", OTHER_CORE)

    slabs = jnp.concatenate([cut(0), after[:per_group], far_a, far_b, before[:per_group]])
    slabs = jnp.roll(slabs.reshape(SIDE, per_group, slab, width), z, axis=0)
    slabs_twin = lax.ppermute(slabs, "aux", OTHER_CORE)

    products = occ_product(own, occ_pieces, (chips, CORES, slab, width), 0)
    products = hold(occ_product(twin, occ_pieces, products, 1), slabs_twin)
    got = lax.all_to_all(
        products, ALL, split_axis=0, concat_axis=0, tiled=True, axis_index_groups=SAME_CORE
    )

    virt = lax.all_gather(virt_rows, "ao", axis=0, tiled=True)
    tensor_slab = jnp.where(
        core == 0, jnp.stack([slabs, slabs_twin], 1), jnp.stack([slabs_twin, slabs], 1)
    ).reshape(-1, slab, width)
    other = lax.dot_general(
        tensor_slab, virt, (((2,), (1,)), ((), ())), preferred_element_type=jnp.float32
    ).astype(jnp.bfloat16)
    other = jnp.transpose(other, (1, 2, 0))

    part = final_product(got, other)
    part = part.reshape(SIDE * SIDE, SIDE, CORES, SIDE * SIDE, -1)
    parcels = jnp.transpose(part, (3, 1, 2, 0, 4)).reshape(chips, -1)
    summed = lax.all_to_all(
        parcels, ALL, split_axis=0, concat_axis=0, tiled=True, axis_index_groups=SAME_CORE
    ).sum(axis=0).reshape(CORES, per_group, -1)
    mine, theirs = summed[0], lax.ppermute(summed[1], "aux", OTHER_CORE)
    return jnp.where(core == 0, jnp.stack([mine, theirs]), jnp.stack([theirs, mine]))


def solution(mesh):
    return jax.shard_map(
        body,
        mesh=mesh,
        in_specs=(
            P("aux", "ao", None),
            P("ao", None),
            P(None, "ao", None),
            P(None, "ao", None),
            P(None, "ao", None),
        ),
        out_specs=P(None, "aux", "ao"),
        check_vma=False,
    )
```

```python
import jax
import jax.numpy as jnp
from jax import lax
from jax.experimental import pallas as pl
from jax.experimental.pallas import tpu as pltpu
from jax.sharding import PartitionSpec as P

ALL = ("ao", "aux")
SIDE = 4
CORES = 2
MIB = 1 << 20
LANES = 128

OTHER_CORE = [(k, k ^ 1) for k in range(SIDE * CORES)]
SAME_CORE = [
    [i * SIDE * CORES + CORES * z + core for i in range(SIDE * SIDE) for z in range(SIDE)]
    for core in range(CORES)
]


def expand(mask_row, width):
    return jnp.repeat(mask_row, width, axis=-1).astype(jnp.bfloat16)


def hold(value, *others):
    def kernel(*refs):
        pass

    whole = pl.BlockSpec(memory_space=pl.ANY)
    return pl.pallas_call(
        kernel,
        out_shape=jax.ShapeDtypeStruct(value.shape, value.dtype),
        in_specs=[whole] * (1 + len(others)),
        out_specs=whole,
        input_output_aliases={0: 0},
    )(value, *others)


def occ_product(occ, matrix, into, index, *others):
    depth, width = matrix.shape
    first = isinstance(into, tuple)
    shape = into if first else into.shape
    columns = width // 2

    def kernel(occ_ref, matrix_ref, *refs):
        product = jnp.dot(occ_ref[0], matrix_ref[...], preferred_element_type=jnp.float32)
        refs[-1][...] = product.astype(jnp.bfloat16).reshape(refs[-1].shape)

    return pl.pallas_call(
        kernel,
        grid=(width // columns,),
        out_shape=jax.ShapeDtypeStruct(shape, jnp.bfloat16),
        in_specs=[
            pl.BlockSpec((1, depth, depth), lambda j: (0, 0, 0)),
            pl.BlockSpec((depth, columns), lambda j: (0, j)),
        ]
        + [pl.BlockSpec(memory_space=pl.ANY)] * (len(others) + (not first)),
        out_specs=pl.BlockSpec((shape[0], 1, shape[2], columns), lambda j: (0, index, 0, j)),
        input_output_aliases={} if first else {2: 0},
        compiler_params=pltpu.CompilerParams(vmem_limit_bytes=56 * MIB),
        cost_estimate=pl.CostEstimate(
            flops=2 * depth * depth * width, bytes_accessed=6 * depth * width, transcendentals=0
        ),
    )(occ, matrix, *([] if first else [into]), *others)


def final_product(got, other):
    sources, pair, slab, width = got.shape
    count = other.shape[-1]
    columns = width // 4

    def kernel(got_ref, other_ref, out_ref, wide):
        total = jnp.zeros(out_ref.shape, jnp.float32)
        for part in range(columns // LANES):
            lanes = pl.ds(part * LANES, LANES)
            wide[part] = got_ref[..., lanes].reshape(wide.shape[1:]).astype(jnp.float32)
        for row in range(slab):
            left = [wide[part, pl.ds(row, sources * pair, stride=slab), :] for part in range(columns // LANES)]
            left = jnp.concatenate(left, 1).astype(jnp.bfloat16)
            total += jnp.dot(left, other_ref[row], preferred_element_type=jnp.float32)

        @pl.when(pl.program_id(0) == 0)
        def _():
            out_ref[...] = jnp.zeros_like(out_ref)

        out_ref[...] += total

    return pl.pallas_call(
        kernel,
        grid=(width // columns,),
        out_shape=jax.ShapeDtypeStruct((sources * pair, count), jnp.float32),
        in_specs=[
            pl.BlockSpec((sources, pair, slab, columns), lambda j: (0, 0, 0, j)),
            pl.BlockSpec((slab, columns, count), lambda j: (0, j, 0)),
        ],
        out_specs=pl.BlockSpec((sources * pair, count), lambda j: (0, 0)),
        scratch_shapes=[pltpu.VMEM((columns // LANES, sources * pair * slab, LANES), jnp.float32)],
        compiler_params=pltpu.CompilerParams(vmem_limit_bytes=56 * MIB),
        cost_estimate=pl.CostEstimate(
            flops=2 * sources * pair * slab * width * count,
            bytes_accessed=2 * got.size + 2 * other.size,
            transcendentals=0,
        ),
    )(got, other)


def body(three_centre, tensor_mask, occ_density, virt_density, density_mask):
    per_group, rows, width = three_centre.shape
    chips = SIDE**3
    slab = width // chips
    core = lax.axis_index("aux") % CORES

    dens_mask = expand(density_mask[:, 0, :], rows)
    row_mask = expand(tensor_mask[0], rows)

    occ_rows = lax.dynamic_index_in_dim(occ_density, core, 0, False) * dens_mask[0][None, :]
    virt_rows = lax.dynamic_index_in_dim(virt_density, core, 0, False) * dens_mask[1][None, :]
    dens = lax.all_gather(jnp.stack([occ_rows, virt_rows]), "ao", axis=1, tiled=True)
    occ, virt = dens[0], dens[1]

    screened = three_centre * row_mask
    own = lax.all_to_all(screened, "ao", split_axis=0, concat_axis=1, tiled=True)[0]
    twin = lax.ppermute(own, "aux", OTHER_CORE)
    groups = lax.axis_size("aux")
    slabs = lax.all_to_all(
        screened.reshape(per_group, groups, -1, width), "aux", split_axis=1, concat_axis=0, tiled=True
    ).reshape(groups * per_group, -1, width)
    slabs_other = lax.ppermute(slabs, "aux", OTHER_CORE)

    products = occ_product(dens, own, (chips, CORES, slab, width), 0)
    products = occ_product(dens, twin, products, 1)
    products = hold(products, slabs)
    got = lax.all_to_all(
        products, ALL, split_axis=0, concat_axis=0, tiled=True, axis_index_groups=SAME_CORE
    )
    tensor_slab = jnp.where(
        core == 0, jnp.concatenate([slabs, slabs_other], 1), jnp.concatenate([slabs_other, slabs], 1)
    )
    other = lax.dot_general(
        tensor_slab, virt, (((2,), (1,)), ((), ())), preferred_element_type=jnp.float32
    ).astype(jnp.bfloat16)
    other = jnp.transpose(other, (1, 2, 0))

    part = final_product(got, other)
    part = part.reshape(SIDE * SIDE, SIDE, CORES, SIDE * SIDE, -1)
    parcels = jnp.transpose(part, (3, 1, 2, 0, 4)).reshape(chips, -1)
    summed = lax.all_to_all(
        parcels, ALL, split_axis=0, concat_axis=0, tiled=True, axis_index_groups=SAME_CORE
    ).sum(axis=0).reshape(CORES, per_group, -1)
    mine, theirs = summed[0], lax.ppermute(summed[1], "aux", OTHER_CORE)
    return jnp.where(core == 0, jnp.stack([mine, theirs]), jnp.stack([theirs, mine]))


def solution(mesh):
    return jax.shard_map(
        body,
        mesh=mesh,
        in_specs=(
            P("aux", "ao", None),
            P("ao", None),
            P(None, "ao", None),
            P(None, "ao", None),
            P(None, "ao", None),
        ),
        out_specs=P(None, "aux", "ao"),
        check_vma=False,
    )
```

```python
import jax
import jax.numpy as jnp
from jax import lax
from jax.experimental import pallas as pl
from jax.experimental.pallas import tpu as pltpu
from jax.sharding import PartitionSpec as P

ALL = ("ao", "aux")
SIDE = 4
CORES = 2
MIB = 1 << 20
LANES = 128

OTHER_CORE = [(k, k ^ 1) for k in range(SIDE * CORES)]
SAME_CORE = [
    [i * SIDE * CORES + CORES * z + core for i in range(SIDE * SIDE) for z in range(SIDE)]
    for core in range(CORES)
]


def expand(mask_row, width):
    return jnp.repeat(mask_row, width, axis=-1).astype(jnp.bfloat16)


def hold(value, *others):
    def kernel(*refs):
        pass

    whole = pl.BlockSpec(memory_space=pl.ANY)
    return pl.pallas_call(
        kernel,
        out_shape=jax.ShapeDtypeStruct(value.shape, value.dtype),
        in_specs=[whole] * (1 + len(others)),
        out_specs=whole,
        input_output_aliases={0: 0},
    )(value, *others)


def occ_product(dens, matrices, slab):
    depth, width = matrices[0].shape
    count, columns = len(matrices), width // 4

    def kernel(occ_ref, *refs):
        for n in range(count):
            product = jnp.dot(occ_ref[0], refs[n][...], preferred_element_type=jnp.float32)
            refs[-1][:, n] = product.astype(jnp.bfloat16).reshape(depth // slab, slab, columns)

    return pl.pallas_call(
        kernel,
        grid=(width // columns,),
        out_shape=jax.ShapeDtypeStruct((depth // slab, count, slab, width), jnp.bfloat16),
        in_specs=[pl.BlockSpec((1, depth, depth), lambda j: (0, 0, 0))]
        + [pl.BlockSpec((depth, columns), lambda j: (0, j))] * count,
        out_specs=pl.BlockSpec((depth // slab, count, slab, columns), lambda j: (0, 0, 0, j)),
        compiler_params=pltpu.CompilerParams(vmem_limit_bytes=56 * MIB),
        cost_estimate=pl.CostEstimate(
            flops=2 * count * depth * depth * width, bytes_accessed=10 * depth * width, transcendentals=0
        ),
    )(dens, *matrices)


def final_product(got, other):
    sources, pair, slab, width = got.shape
    count = other.shape[-1]
    columns = width // 4

    def kernel(got_ref, other_ref, out_ref, wide):
        for part in range(columns // LANES):
            lanes = pl.ds(part * LANES, LANES)
            wide[part] = got_ref[..., lanes].reshape(wide.shape[1:]).astype(jnp.float32)
        left = [
            wide[part, pl.ds(row, sources * pair, stride=slab), :].astype(jnp.bfloat16)
            for row in range(slab)
            for part in range(columns // LANES)
        ]
        right = other_ref[...].reshape(slab * columns, count)
        total = jnp.dot(jnp.concatenate(left, 1), right, preferred_element_type=jnp.float32)

        @pl.when(pl.program_id(0) == 0)
        def _():
            out_ref[...] = jnp.zeros_like(out_ref)

        out_ref[...] += total

    return pl.pallas_call(
        kernel,
        grid=(width // columns,),
        out_shape=jax.ShapeDtypeStruct((sources * pair, count), jnp.float32),
        in_specs=[
            pl.BlockSpec((sources, pair, slab, columns), lambda j: (0, 0, 0, j)),
            pl.BlockSpec((slab, columns, count), lambda j: (0, j, 0)),
        ],
        out_specs=pl.BlockSpec((sources * pair, count), lambda j: (0, 0)),
        scratch_shapes=[pltpu.VMEM((columns // LANES, sources * pair * slab, LANES), jnp.float32)],
        compiler_params=pltpu.CompilerParams(vmem_limit_bytes=56 * MIB),
        cost_estimate=pl.CostEstimate(
            flops=2 * sources * pair * slab * width * count,
            bytes_accessed=2 * got.size + 2 * other.size,
            transcendentals=0,
        ),
    )(got, other)


def body(three_centre, tensor_mask, occ_density, virt_density, density_mask):
    per_group, rows, width = three_centre.shape
    chips = SIDE**3
    slab = width // chips
    core = lax.axis_index("aux") % CORES

    dens_mask = expand(density_mask[:, 0, :], rows)
    row_mask = expand(tensor_mask[0], rows)

    occ_rows = lax.dynamic_index_in_dim(occ_density, core, 0, False) * dens_mask[0][None, :]
    virt_rows = lax.dynamic_index_in_dim(virt_density, core, 0, False) * dens_mask[1][None, :]
    dens = lax.all_gather(jnp.stack([occ_rows, virt_rows]), "ao", axis=1, tiled=True)
    occ, virt = dens[0], dens[1]

    screened = three_centre * row_mask
    own = lax.all_to_all(screened, "ao", split_axis=0, concat_axis=1, tiled=True)[0]
    twin = lax.ppermute(own, "aux", OTHER_CORE)
    groups = lax.axis_size("aux")
    slabs = lax.all_to_all(
        screened.reshape(per_group, groups, -1, width), "aux", split_axis=1, concat_axis=0, tiled=True
    ).reshape(groups * per_group, -1, width)
    slabs_other = lax.ppermute(slabs, "aux", OTHER_CORE)

    products = occ_product(dens, (own, twin), slab)
    products = hold(products, slabs)
    got = lax.all_to_all(
        products, ALL, split_axis=0, concat_axis=0, tiled=True, axis_index_groups=SAME_CORE
    )
    tensor_slab = jnp.where(
        core == 0, jnp.concatenate([slabs, slabs_other], 1), jnp.concatenate([slabs_other, slabs], 1)
    )
    other = lax.dot_general(
        tensor_slab, virt, (((2,), (1,)), ((), ())), preferred_element_type=jnp.float32
    ).astype(jnp.bfloat16)
    other = jnp.transpose(other, (1, 2, 0))

    part = final_product(got, other)
    part = part.reshape(SIDE * SIDE, SIDE, CORES, SIDE * SIDE, -1)
    part = jnp.where(core == 0, part, part[:, :, ::-1])
    parcels = jnp.transpose(part, (3, 1, 2, 0, 4)).reshape(chips * CORES, -1)
    parts = lax.all_to_all(parcels, ALL, split_axis=0, concat_axis=0, tiled=True)
    return parts.reshape(chips, CORES, -1).sum(axis=0).reshape(CORES, per_group, -1)


def solution(mesh):
    return jax.shard_map(
        body,
        mesh=mesh,
        in_specs=(
            P("aux", "ao", None),
            P("ao", None),
            P(None, "ao", None),
            P(None, "ao", None),
            P(None, "ao", None),
        ),
        out_specs=P(None, "aux", "ao"),
        check_vma=False,
    )
```

```python
import jax
import jax.numpy as jnp
from jax import lax
from jax.experimental import pallas as pl
from jax.experimental.pallas import tpu as pltpu
from jax.sharding import PartitionSpec as P

ALL = ("ao", "aux")
SIDE = 4
CORES = 2
MIB = 1 << 20
LANES = 128

OTHER_CORE = [(k, k ^ 1) for k in range(SIDE * CORES)]
SAME_CORE = [
    [i * SIDE * CORES + CORES * z + core for i in range(SIDE * SIDE) for z in range(SIDE)]
    for core in range(CORES)
]


def expand(mask_row, width):
    return jnp.repeat(mask_row, width, axis=-1).astype(jnp.bfloat16)


def occ_product(dens, matrices, slab):
    depth, width = matrices[0].shape
    count, columns = len(matrices), width // 4

    def kernel(occ_ref, *refs):
        for n in range(count):
            product = jnp.dot(occ_ref[0], refs[n][...], preferred_element_type=jnp.float32)
            refs[-1][:, n] = product.astype(jnp.bfloat16).reshape(depth // slab, slab, columns)

    return pl.pallas_call(
        kernel,
        grid=(width // columns,),
        out_shape=jax.ShapeDtypeStruct((depth // slab, count, slab, width), jnp.bfloat16),
        in_specs=[pl.BlockSpec((1, depth, depth), lambda j: (0, 0, 0))]
        + [pl.BlockSpec((depth, columns), lambda j: (0, j))] * count,
        out_specs=pl.BlockSpec((depth // slab, count, slab, columns), lambda j: (0, 0, 0, j)),
        compiler_params=pltpu.CompilerParams(vmem_limit_bytes=56 * MIB),
        cost_estimate=pl.CostEstimate(
            flops=2 * count * depth * depth * width, bytes_accessed=10 * depth * width, transcendentals=0
        ),
    )(dens, *matrices)


def final_product(got, other):
    sources, pair, slab, width = got.shape
    count = other.shape[-1]
    columns = width // 4

    def kernel(got_ref, other_ref, out_ref, wide):
        for part in range(columns // LANES):
            lanes = pl.ds(part * LANES, LANES)
            wide[part] = got_ref[..., lanes].reshape(wide.shape[1:]).astype(jnp.float32)
        left = [
            wide[part, pl.ds(row, sources * pair, stride=slab), :].astype(jnp.bfloat16)
            for row in range(slab)
            for part in range(columns // LANES)
        ]
        right = other_ref[...].reshape(slab * columns, count)
        total = jnp.dot(jnp.concatenate(left, 1), right, preferred_element_type=jnp.float32)

        @pl.when(pl.program_id(0) == 0)
        def _():
            out_ref[...] = jnp.zeros_like(out_ref)

        out_ref[...] += total

    return pl.pallas_call(
        kernel,
        grid=(width // columns,),
        out_shape=jax.ShapeDtypeStruct((sources * pair, count), jnp.float32),
        in_specs=[
            pl.BlockSpec((sources, pair, slab, columns), lambda j: (0, 0, 0, j)),
            pl.BlockSpec((slab, columns, count), lambda j: (0, j, 0)),
        ],
        out_specs=pl.BlockSpec((sources * pair, count), lambda j: (0, 0)),
        scratch_shapes=[pltpu.VMEM((columns // LANES, sources * pair * slab, LANES), jnp.float32)],
        compiler_params=pltpu.CompilerParams(vmem_limit_bytes=56 * MIB),
        cost_estimate=pl.CostEstimate(
            flops=2 * sources * pair * slab * width * count,
            bytes_accessed=2 * got.size + 2 * other.size,
            transcendentals=0,
        ),
    )(got, other)


def body(three_centre, tensor_mask, occ_density, virt_density, density_mask):
    per_group, rows, width = three_centre.shape
    chips = SIDE**3
    slab = width // chips
    core = lax.axis_index("aux") % CORES

    dens_mask = expand(density_mask[:, 0, :], rows)
    row_mask = expand(tensor_mask[0], rows)

    occ_rows = lax.dynamic_index_in_dim(occ_density, core, 0, False) * dens_mask[0][None, :]
    virt_rows = lax.dynamic_index_in_dim(virt_density, core, 0, False) * dens_mask[1][None, :]
    dens = lax.all_gather(jnp.stack([occ_rows, virt_rows]), "ao", axis=1, tiled=True)
    occ, virt = dens[0], dens[1]

    screened = three_centre * row_mask
    own = lax.all_to_all(screened, "ao", split_axis=0, concat_axis=1, tiled=True)[0]
    twin = lax.ppermute(own, "aux", OTHER_CORE)
    groups = lax.axis_size("aux")
    slabs = lax.all_to_all(
        screened.reshape(per_group, groups, -1, width), "aux", split_axis=1, concat_axis=0, tiled=True
    ).reshape(groups * per_group, -1, width)
    slabs_other = lax.ppermute(slabs, "aux", OTHER_CORE)

    products = occ_product(dens, (own, twin), slab)
    got = lax.all_to_all(
        products, ALL, split_axis=0, concat_axis=0, tiled=True, axis_index_groups=SAME_CORE
    )
    tensor_slab = jnp.where(
        core == 0, jnp.concatenate([slabs, slabs_other], 1), jnp.concatenate([slabs_other, slabs], 1)
    )
    other = lax.dot_general(
        tensor_slab, virt, (((2,), (1,)), ((), ())), preferred_element_type=jnp.float32
    ).astype(jnp.bfloat16)
    other = jnp.transpose(other, (1, 2, 0))

    part = final_product(got, other)
    part = part.reshape(SIDE * SIDE, SIDE, CORES, SIDE * SIDE, -1)
    part = jnp.where(core == 0, part, part[:, :, ::-1])
    parcels = jnp.transpose(part, (3, 1, 2, 0, 4)).reshape(chips * CORES, -1)
    parts = lax.all_to_all(parcels, ALL, split_axis=0, concat_axis=0, tiled=True)
    return parts.reshape(chips, CORES, -1).sum(axis=0).reshape(CORES, per_group, -1)


def solution(mesh):
    return jax.shard_map(
        body,
        mesh=mesh,
        in_specs=(
            P("aux", "ao", None),
            P("ao", None),
            P(None, "ao", None),
            P(None, "ao", None),
            P(None, "ao", None),
        ),
        out_specs=P(None, "aux", "ao"),
        check_vma=False,
    )
```

```python
import jax
import jax.numpy as jnp
from jax import lax
from jax.experimental import pallas as pl
from jax.experimental.pallas import tpu as pltpu
from jax.sharding import PartitionSpec as P

ALL = ("ao", "aux")
SIDE = 4
CORES = 2
MIB = 1 << 20
LANES = 128

OTHER_CORE = [(k, k ^ 1) for k in range(SIDE * CORES)]
SAME_CORE = [
    [i * SIDE * CORES + CORES * z + core for i in range(SIDE * SIDE) for z in range(SIDE)]
    for core in range(CORES)
]


def expand(mask_row, width):
    return jnp.repeat(mask_row, width, axis=-1).astype(jnp.bfloat16)


def occ_product(dens, matrices, slab):
    depth, width = matrices[0].shape
    count, columns = len(matrices), width // 2

    def kernel(occ_ref, *refs):
        for n in range(count):
            product = jnp.dot(occ_ref[0], refs[n][...], preferred_element_type=jnp.float32)
            refs[-1][:, n] = product.astype(jnp.bfloat16).reshape(depth // slab, slab, columns)

    return pl.pallas_call(
        kernel,
        grid=(width // columns,),
        out_shape=jax.ShapeDtypeStruct((depth // slab, count, slab, width), jnp.bfloat16),
        in_specs=[pl.BlockSpec((1, depth, depth), lambda j: (0, 0, 0))]
        + [pl.BlockSpec((depth, columns), lambda j: (0, j))] * count,
        out_specs=pl.BlockSpec((depth // slab, count, slab, columns), lambda j: (0, 0, 0, j)),
        compiler_params=pltpu.CompilerParams(vmem_limit_bytes=56 * MIB),
        cost_estimate=pl.CostEstimate(
            flops=2 * count * depth * depth * width, bytes_accessed=10 * depth * width, transcendentals=0
        ),
    )(dens, *matrices)


def final_product(got, other):
    sources, pair, slab, width = got.shape
    count = other.shape[-1]
    columns = width // 4

    def kernel(got_ref, other_ref, out_ref, wide):
        for part in range(columns // LANES):
            lanes = pl.ds(part * LANES, LANES)
            wide[part] = got_ref[..., lanes].reshape(wide.shape[1:]).astype(jnp.float32)
        left = [
            wide[part, pl.ds(row, sources * pair, stride=slab), :].astype(jnp.bfloat16)
            for row in range(slab)
            for part in range(columns // LANES)
        ]
        right = other_ref[...].reshape(slab * columns, count)
        total = jnp.dot(jnp.concatenate(left, 1), right, preferred_element_type=jnp.float32)

        @pl.when(pl.program_id(0) == 0)
        def _():
            out_ref[...] = jnp.zeros_like(out_ref)

        out_ref[...] += total

    return pl.pallas_call(
        kernel,
        grid=(width // columns,),
        out_shape=jax.ShapeDtypeStruct((sources * pair, count), jnp.float32),
        in_specs=[
            pl.BlockSpec((sources, pair, slab, columns), lambda j: (0, 0, 0, j)),
            pl.BlockSpec((slab, columns, count), lambda j: (0, j, 0)),
        ],
        out_specs=pl.BlockSpec((sources * pair, count), lambda j: (0, 0)),
        scratch_shapes=[pltpu.VMEM((columns // LANES, sources * pair * slab, LANES), jnp.float32)],
        compiler_params=pltpu.CompilerParams(vmem_limit_bytes=56 * MIB),
        cost_estimate=pl.CostEstimate(
            flops=2 * sources * pair * slab * width * count,
            bytes_accessed=2 * got.size + 2 * other.size,
            transcendentals=0,
        ),
    )(got, other)


def body(three_centre, tensor_mask, occ_density, virt_density, density_mask):
    per_group, rows, width = three_centre.shape
    chips = SIDE**3
    slab = width // chips
    core = lax.axis_index("aux") % CORES

    dens_mask = expand(density_mask[:, 0, :], rows)
    row_mask = expand(tensor_mask[0], rows)

    occ_rows = lax.dynamic_index_in_dim(occ_density, core, 0, False) * dens_mask[0][None, :]
    virt_rows = lax.dynamic_index_in_dim(virt_density, core, 0, False) * dens_mask[1][None, :]
    dens = lax.all_gather(jnp.stack([occ_rows, virt_rows]), "ao", axis=1, tiled=True)
    occ, virt = dens[0], dens[1]

    screened = three_centre * row_mask
    own = lax.all_to_all(screened, "ao", split_axis=0, concat_axis=1, tiled=True)[0]
    twin = lax.ppermute(own, "aux", OTHER_CORE)
    groups = lax.axis_size("aux")
    slabs = lax.all_to_all(
        screened.reshape(per_group, groups, -1, width), "aux", split_axis=1, concat_axis=0, tiled=True
    ).reshape(groups * per_group, -1, width)
    slabs_other = lax.ppermute(slabs, "aux", OTHER_CORE)

    products = occ_product(dens, (own, twin), slab)
    got = lax.all_to_all(
        products, ALL, split_axis=0, concat_axis=0, tiled=True, axis_index_groups=SAME_CORE
    )
    tensor_slab = jnp.where(
        core == 0, jnp.concatenate([slabs, slabs_other], 1), jnp.concatenate([slabs_other, slabs], 1)
    )
    other = lax.dot_general(
        tensor_slab, virt, (((2,), (1,)), ((), ())), preferred_element_type=jnp.float32
    ).astype(jnp.bfloat16)
    other = jnp.transpose(other, (1, 2, 0))

    part = final_product(got, other)
    part = part.reshape(SIDE * SIDE, SIDE, CORES, SIDE * SIDE, -1)
    part = jnp.where(core == 0, part, part[:, :, ::-1])
    parcels = jnp.transpose(part, (3, 1, 2, 0, 4)).reshape(chips * CORES, -1)
    parts = lax.all_to_all(parcels, ALL, split_axis=0, concat_axis=0, tiled=True)
    return parts.reshape(chips, CORES, -1).sum(axis=0).reshape(CORES, per_group, -1)


def solution(mesh):
    return jax.shard_map(
        body,
        mesh=mesh,
        in_specs=(
            P("aux", "ao", None),
            P("ao", None),
            P(None, "ao", None),
            P(None, "ao", None),
            P(None, "ao", None),
        ),
        out_specs=P(None, "aux", "ao"),
        check_vma=False,
    )
```
